128 devices in a mesh: row: 8 (over x, y_lo), col: 16 (over y_hi, z, core).
Axes of the slice: x: 4, y: 4 (y_hi: 2, y_lo: 2; y = y_hi * 2 + y_lo), z: 4, core: 2. Of those that a mesh axis runs over, the one named last changes fastest.
Arguments:
- tokens: bfloat16 [1024, 6144], P('row', 'col'), may hold values from -6 to 6
- w_in: bfloat16 [6144, 24576], P('col', 'row'), may hold values from -0.078125 to 0.078125
- w_out: bfloat16 [24576, 6144], P('row', 'col'), may hold values from -0.0390625 to 0.0390625
- out_grad: bfloat16 [1024, 6144], P('row', 'col'), may hold values from -6 to 6
Outputs:
- in_grad: bfloat16 [1024, 6144], P('row', 'col')
- w_in_grad: float32 [6144, 24576], P('col', 'row')
- w_out_grad: float32 [24576, 6144], P('row', 'col')
The draws below stay inside these ranges and needn't reach their ends.
All inputs are finite; a program needn't handle non-finite values.
Results may differ from the reference program's by a relative error of at most 0.028.
Values may be sent and summed in bfloat16 or wider, within the bound.
No kernel may reach another device: no remote copies, remote signals or barrier semaphores. Data moves between devices by JAX's collectives and lax.ppermute only.
A program may use at most 128 MiB of HBM per device.

```python
import jax
import jax.numpy as jnp
from jax import lax

D = 6144
FF = 24576
TOKENS = 1024
N_COL = 16


def steps_of(rng, shape, cuts, smallest, largest):
    def one(position, parts):
        heights = jax.random.uniform(jax.random.fold_in(jax.random.fold_in(rng, 6), position), (parts,), jnp.float32, smallest / len(cuts), largest / len(cuts))
        return jnp.repeat(jnp.exp(heights), shape[position] // parts).reshape((-1,) + (1,) * (len(shape) - position - 1))

    factor_of = one(*cuts[0])
    for cut in cuts[1:]:
        factor_of = factor_of * one(*cut)
    return factor_of


def noise(rng, shape, scale, bound, pieces=(), kind=jnp.bfloat16):
    gain = steps_of(rng, shape, pieces, -0.22, 0.18) if pieces else 1.0
    values = jax.random.normal(rng, shape, jnp.float32) * scale * gain
    return jnp.minimum(jnp.maximum(values, -bound), bound).astype(kind)


def setup_inputs(seed: int = 0) -> dict:
    key_of = jax.random.split(jax.random.key(seed), 5)
    return {
        "tokens": noise(key_of[0], (TOKENS, D), 1.0, 6.0, ((0, 8), (1, 16))),
        "w_in": noise(key_of[1], (D, FF), D ** -0.5, 0.078125, ((0, 16), (1, 8))),
        "w_out": noise(key_of[2], (FF, D), FF ** -0.5, 0.0390625, ((0, 8), (1, 16))),
        "out_grad": noise(key_of[3], (TOKENS, D), 1.0, 6.0, ((0, 8), (1, 16))),
    }


inv_root_two = 0.7071067811865476
inv_root_two_pi = 0.3989422804014327


def gelu_value(values):
    return 0.5 * values * (1.0 + jax.scipy.special.erf(values * inv_root_two))


def gelu_slope(values):
    return 0.5 * (1.0 + jax.scipy.special.erf(values * inv_root_two)) + values * jnp.exp(-0.5 * values * values) * inv_root_two_pi


def block_sum(left, right, blocks):
    width = left.shape[1] // blocks

    def advance(total, block_index):
        offset = (block_index * width).astype(jnp.int32)
        left_part = lax.dynamic_slice_in_dim(left, offset, width, 1)
        right_part = lax.dynamic_slice_in_dim(right, offset, width, 0)
        term = jnp.dot(left_part, right_part, preferred_element_type=jnp.float32)
        rounded = lax.optimization_barrier(term.astype(jnp.bfloat16))
        return total + rounded.astype(jnp.float32), None

    start_total = jnp.zeros((left.shape[0], right.shape[1]), jnp.float32)
    total, _ = lax.scan(advance, start_total, jnp.arange(blocks, dtype=jnp.int32))
    return total


def reference(tokens, w_in, w_out, out_grad):
    hidden = block_sum(tokens, w_in, N_COL)
    gelu_out = gelu_value(hidden).astype(jnp.bfloat16)
    w_out_grad = lax.dot_general(gelu_out, out_grad, (((0,), (0,)), ((), ())), preferred_element_type=jnp.float32)
    hidden_grad = block_sum(out_grad, jnp.transpose(w_out), N_COL)
    pre_grad = (hidden_grad * gelu_slope(hidden)).astype(jnp.bfloat16)
    w_in_grad = lax.dot_general(tokens, pre_grad, (((0,), (0,)), ((), ())), preferred_element_type=jnp.float32)
    in_grad = lax.dot_general(pre_grad, w_in, (((1,), (1,)), ((), ())), preferred_element_type=jnp.float32).astype(jnp.bfloat16)
    return in_grad, w_in_grad, w_out_grad
```

```python
import jax
import jax.numpy as jnp
from jax import lax
from jax.sharding import PartitionSpec as P

inv_root_two = 0.7071067811865476
inv_root_two_pi = 0.3989422804014327
AXES = ("row", "col")


def gelu_value(values):
    return 0.5 * values * (1.0 + jax.scipy.special.erf(values * inv_root_two))


def gelu_slope(values):
    return (
        0.5 * (1.0 + jax.scipy.special.erf(values * inv_root_two))
        + values * jnp.exp(-0.5 * values * values) * inv_root_two_pi
    )


def device_index(x, y, z, core):
    return (x * 2 + y % 2) * 16 + (y // 2) * 8 + z * 2 + core


def flip_pairs(x_flip=0, y_flip=0, z_flip=0, core_flip=0):
    return [
        (
            device_index(x, y, z, core),
            device_index(x ^ x_flip, y ^ y_flip, z ^ z_flip, core ^ core_flip),
        )
        for x in range(4)
        for y in range(4)
        for z in range(4)
        for core in range(2)
    ]


FLIPS = {
    "a": flip_pairs(z_flip=1),
    "b": flip_pairs(z_flip=3),
    "y": flip_pairs(y_flip=2),
    "core": flip_pairs(core_flip=1),
}
ROW_FLIPS = [
    flip_pairs(x_flip=xa ^ (3 * xb), y_flip=yl) for xa in range(2) for xb in range(2) for yl in range(2)
]
STREAMS = ("yab", "yba", "aby", "bay")


def swap(values, name):
    return lax.ppermute(values, AXES, FLIPS[name])


def relative(values, bits):
    rows, width = values.shape
    pieces = values.reshape(2, 2, 2, rows // 8, width)
    for axis, bit in enumerate(bits):
        pieces = jnp.where(bit == 1, jnp.flip(pieces, axis), pieces)
    return pieces.reshape(rows, width)


def to_stream(blocks, order):
    rows, width = blocks[0].shape
    pieces = jnp.stack(blocks).reshape(2, 2, 2, 2, rows // 8, width)
    axes = ["aby".index(letter) + 1 for letter in order]
    return pieces.transpose(*axes, 0, 4, 5).reshape(2 * rows, width)


def from_stream(values, order):
    rows, width = values.shape
    pieces = values.reshape(2, 2, 2, 2, rows // 16, width)
    place = [order.index(letter) for letter in "aby"]
    pieces = pieces.transpose(3, *place, 4, 5)
    return [pieces[i].reshape(rows // 2, width) for i in range(2)]


def gather_row(block):
    return [block] + [lax.ppermute(block, AXES, pairs) for pairs in ROW_FLIPS[1:]]


def streams_of(block):
    blocks = gather_row(block)
    return [to_stream(blocks[2 * i : 2 * i + 2], order) for i, order in enumerate(STREAMS)]


def reduce_streams(streams, weight, dot):
    half = streams[0].shape[0] // 2
    first = jnp.concatenate([s[half:] for s in streams])
    keep = jnp.concatenate([s[:half] for s in streams])
    sent = dot(first, weight).astype(jnp.bfloat16)
    got_y = swap(sent[: 2 * half], "y")
    got = [
        got_y[:half],
        got_y[half:],
        swap(sent[2 * half : 3 * half], "a"),
        swap(sent[3 * half :], "b"),
    ]
    kept = dot(keep, weight)
    out = []
    q = half // 4
    for i, order in enumerate(STREAMS):
        k = kept[i * half : (i + 1) * half]
        r1 = got[i].astype(jnp.float32)
        second = (k[2 * q :] + r1[2 * q :]).astype(jnp.bfloat16)
        r2 = swap(second, order[1]).astype(jnp.float32)
        third = (k[q : 2 * q] + r1[q : 2 * q] + r2[q:]).astype(jnp.bfloat16)
        r3 = swap(third, order[2]).astype(jnp.float32)
        out.append(k[:q] + r1[:q] + r2[:q] + r3)
    return out


def gather_streams(shares, core):
    pieces = []
    keeps = []
    for share, order in zip(shares, STREAMS):
        two = jnp.concatenate([share, swap(share, order[2])])
        keeps.append(jnp.concatenate([two, swap(two, order[1])]))
    got_y = swap(jnp.concatenate(keeps[:2]), "y")
    half = keeps[0].shape[0]
    got = [got_y[:half], got_y[half:], swap(keeps[2], "a"), swap(keeps[3], "b")]
    for keep, first in zip(keeps, got):
        for piece in (keep, first):
            other = swap(piece, "core")
            pieces.append((piece, other))
    mine = jnp.concatenate([p for p, _ in pieces])
    other = jnp.concatenate([o for _, o in pieces])
    left = jnp.where(core == 0, mine, other)
    right = jnp.where(core == 0, other, mine)
    return jnp.concatenate([left, right], axis=1)


def body(tokens, w_in, w_out, out_grad):
    column = lax.axis_index("col")
    core, z, y_hi = column % 2, (column // 2) % 4, column // 8
    bits = ((z ^ (z >> 1)) & 1, z >> 1, y_hi)
    width = w_in.shape[1] // 2

    def both_cores(values):
        return jnp.concatenate([values, swap(values, "core")], axis=1)

    w_in_mine = lax.dynamic_slice_in_dim(w_in, core * width, width, 1)
    w_in_other = swap(lax.dynamic_slice_in_dim(w_in, (1 - core) * width, width, 1), "core")
    w_in_half = jnp.concatenate([w_in_mine, w_in_other])
    w_out_mine = lax.dynamic_slice_in_dim(w_out, core * width, width, 0)
    w_out_other = swap(lax.dynamic_slice_in_dim(w_out, (1 - core) * width, width, 0), "core")
    w_out_half = jnp.concatenate([w_out_mine, w_out_other], axis=1)

    tok_own = streams_of(relative(tokens, bits))
    tok_rows = jnp.concatenate(tok_own)
    rows = tok_own[0].shape[0]
    tok_all = both_cores(tok_rows)
    grad_own = streams_of(relative(out_grad, bits))
    grad_rows = jnp.concatenate(grad_own)
    grad_all = both_cores(grad_rows)

    hidden = reduce_streams(
        [tok_all[i * rows : (i + 1) * rows] for i in range(4)],
        w_in_half,
        lambda left, right: jnp.dot(left, right, preferred_element_type=jnp.float32),
    )
    hidden_grad = reduce_streams(
        [grad_all[i * rows : (i + 1) * rows] for i in range(4)],
        w_out_half,
        lambda left, right: lax.dot_general(
            left, right, (((1,), (1,)), ((), ())), preferred_element_type=jnp.float32
        ),
    )
    pre_share = [(g * gelu_slope(h)).astype(jnp.bfloat16) for g, h in zip(hidden_grad, hidden)]
    gelu_share = [gelu_value(h).astype(jnp.bfloat16) for h in hidden]
    pre_grad = gather_streams(pre_share, core)
    in_part = lax.dot_general(
        pre_grad, w_in, (((1,), (1,)), ((), ())), preferred_element_type=jnp.float32
    ).astype(jnp.bfloat16)
    blocks = []
    for i, order in enumerate(STREAMS):
        blocks += from_stream(in_part[i * rows : (i + 1) * rows], order)
    total = blocks[0].astype(jnp.float32)
    for block, pairs in zip(blocks[1:], ROW_FLIPS[1:]):
        total = total + lax.ppermute(block, AXES, pairs).astype(jnp.float32)
    in_grad = relative(total, bits).astype(jnp.bfloat16)
    w_in_grad = lax.dot_general(
        tok_rows, pre_grad, (((0,), (0,)), ((), ())), preferred_element_type=jnp.float32
    )
    gelu_out = gather_streams(gelu_share, core)
    w_out_grad = lax.dot_general(
        gelu_out, grad_rows, (((0,), (0,)), ((), ())), preferred_element_type=jnp.float32
    )
    return (in_grad, w_in_grad, w_out_grad)


def solution(mesh):
    in_specs = (P("row", "col"), P("col", "row"), P("row", "col"), P("row", "col"))
    out_specs = (P("row", "col"), P("col", "row"), P("row", "col"))
    return jax.shard_map(body, mesh=mesh, in_specs=in_specs, out_specs=out_specs, check_vma=False)
```

```python
import jax
import jax.numpy as jnp
from jax import lax
from jax.experimental import pallas as pl
from jax.experimental.pallas import tpu as pltpu
from jax.sharding import PartitionSpec as P

inv_root_two = 0.7071067811865476
inv_root_two_pi = 0.3989422804014327
AXES = ("row", "col")


def gelu_value(values):
    return 0.5 * values * (1.0 + jax.scipy.special.erf(values * inv_root_two))


def gelu_slope(values):
    return (
        0.5 * (1.0 + jax.scipy.special.erf(values * inv_root_two))
        + values * jnp.exp(-0.5 * values * values) * inv_root_two_pi
    )


def device_index(x, y, z, core):
    return (x * 2 + y % 2) * 16 + (y // 2) * 8 + z * 2 + core


def flip_pairs(x_flip=0, y_flip=0, z_flip=0, core_flip=0):
    return [
        (
            device_index(x, y, z, core),
            device_index(x ^ x_flip, y ^ y_flip, z ^ z_flip, core ^ core_flip),
        )
        for x in range(4)
        for y in range(4)
        for z in range(4)
        for core in range(2)
    ]


FLIPS = {
    "a": flip_pairs(z_flip=1),
    "b": flip_pairs(z_flip=3),
    "y": flip_pairs(y_flip=2),
    "core": flip_pairs(core_flip=1),
    "xa": flip_pairs(x_flip=1),
    "xb": flip_pairs(x_flip=3),
    "yl": flip_pairs(y_flip=1),
}
TOKEN_ORDERS = ("aby", "bay")
Z_GROUPS = [[y * 8 + z * 2 + core for z in range(4)] for y in range(2) for core in range(2)]


def swap(values, name):
    return lax.ppermute(values, AXES, FLIPS[name])


def after(first, then):
    return lax.optimization_barrier((first, then))[1]


def f32(values):
    return values.astype(jnp.float32)


def b16(values):
    return values.astype(jnp.bfloat16)


TILE = 512
VMEM_LIMIT = 16 * 1024 * 1024
CORE, Z, Y_HI, ROW = range(4)
IN_VMEM = pl.BlockSpec(memory_space=pltpu.VMEM)


def kernel_call(kernel, place, args, out_specs, out_shape, scratch=()):
    return pl.pallas_call(
        kernel,
        in_specs=[pl.BlockSpec(memory_space=pltpu.SMEM)] + [IN_VMEM] * len(args),
        out_specs=out_specs,
        out_shape=out_shape,
        scratch_shapes=scratch,
        compiler_params=pltpu.CompilerParams(vmem_limit_bytes=VMEM_LIMIT),
        cost_estimate=pl.CostEstimate(flops=0, bytes_accessed=0, transcendentals=0),
    )(place, *args)


def copies_for_row(place, out_grad, tokens):
    rows, depth = tokens.shape
    own = rows // 8

    def kernel(place_ref, grad_ref, tok_ref, out_ref):
        z, y_hi = place_ref[Z], place_ref[Y_HI]
        for i in range(8):
            first, second, third = i >> 2, (i >> 1) & 1, i & 1
            grad = grad_ref[(i & 3) * 2 + (y_hi ^ first)]
            tok = tok_ref[(z ^ first ^ (3 * second)) * 2 + (y_hi ^ third)]
            for to in range(8):
                out_ref[to, 0, i * own : (i + 1) * own] = grad
                out_ref[to, 1, i * own : (i + 1) * own] = tok

    pieces = (8, own, depth)
    out = (8, 2, rows, depth)
    return kernel_call(
        kernel,
        place,
        (out_grad.reshape(pieces), tokens.reshape(pieces)),
        IN_VMEM,
        jax.ShapeDtypeStruct(out, tokens.dtype),
    )


def grad_pieces(block):
    return [(block + r, 4 * y + z) for y in range(2) for z in range(4) for r in range(4)]


def token_pieces(chunk, block):
    return [
        (block + r, (first * 4 + second * 2 if chunk == 0 else second * 4 + first * 2) + y)
        for first in range(2)
        for second in range(2)
        for y in range(2)
        for r in range(4)
    ]


def partial_sums(place, raw, raw_other, kind, pieces, weight, weight_other, hidden_axis):
    rows, depth = raw.shape[2:]
    own = rows // 8
    total_rows = own * len(pieces)
    half = total_rows // 2
    width = weight_other.shape[hidden_axis]
    tile = min(TILE, width)
    dims = (((1,), (1 - hidden_axis,)), ((), ()))

    def kernel(place_ref, l_ref, lo_ref, w_ref, wo_ref, keep_ref, send_ref, left):
        for i, (block, piece) in enumerate(pieces):
            left[i * own : (i + 1) * own, :depth] = l_ref[block, kind, piece * own : (piece + 1) * own]
            left[i * own : (i + 1) * own, depth:] = lo_ref[block, kind, piece * own : (piece + 1) * own]
        for start in range(0, width, tile):
            mine = pl.ds(pl.multiple_of(place_ref[CORE] * width + start, tile), tile)
            if hidden_axis == 1:
                right = jnp.concatenate([w_ref[:, mine], wo_ref[:, start : start + tile]])
            else:
                right = jnp.concatenate([w_ref[mine, :], wo_ref[start : start + tile, :]], axis=1)
            total = lax.dot_general(left[...], right, dims, preferred_element_type=jnp.float32)
            total = total.astype(jnp.bfloat16)
            keep_ref[:, start : start + tile] = total[:half]
            send_ref[:, start : start + tile] = total[half:]

    out = jax.ShapeDtypeStruct((half, width), jnp.bfloat16)
    return kernel_call(
        kernel,
        place,
        (raw, raw_other, weight, weight_other),
        [IN_VMEM, IN_VMEM],
        [out, out],
        [pltpu.VMEM((total_rows, 2 * depth), jnp.bfloat16)],
    )


def input_total(place, parts):
    count, rows, depth = parts.shape
    own = rows // 8

    def kernel(place_ref, parts_ref, out_ref):
        z, y_hi = place_ref[Z], place_ref[Y_HI]
        swapped = place_ref[ROW] >= 4
        for i in range(8):
            first, second, y = i >> 2, (i >> 1) & 1, i & 1
            total = parts_ref[0, i * own : (i + 1) * own].astype(jnp.float32)
            for device in range(1, count):
                total += parts_ref[device, i * own : (i + 1) * own].astype(jnp.float32)
            a = jnp.where(swapped, second, first)
            b = jnp.where(swapped, first, second)
            out_ref[(z ^ a ^ (3 * b)) * 2 + (y_hi ^ y)] = total.astype(jnp.bfloat16)

    out = jax.ShapeDtypeStruct((8, own, depth), jnp.bfloat16)
    return kernel_call(kernel, place, (parts,), IN_VMEM, out).reshape(8 * own, depth)


def for_tiles(width, step):
    tile = min(128, width)

    @pl.loop(0, width // tile)
    def _(i):
        step(pl.ds(pl.multiple_of(i * tile, tile), tile))


def fold(place, kept, got, second):
    count = len(kept)
    rows, width = second[0].shape
    half = rows // 2

    def kernel(place_ref, *refs):
        own_ref, send_ref = refs[3 * count :]

        def step(at):
            for i in range(count):
                k, g, s = refs[i], refs[count + i], refs[2 * count + i]
                total = k[:rows, at].astype(jnp.float32) + g[:rows, at].astype(jnp.float32)
                total += s[:, at].astype(jnp.float32)
                own_ref[i * half : (i + 1) * half, at] = total[:half]
                send_ref[i * half : (i + 1) * half, at] = total[half:].astype(jnp.bfloat16)

        for_tiles(width, step)

    out = (count * half, width)
    return kernel_call(
        kernel,
        place,
        (*kept, *got, *second),
        [IN_VMEM, IN_VMEM],
        [jax.ShapeDtypeStruct(out, jnp.float32), jax.ShapeDtypeStruct(out, jnp.bfloat16)],
    )


def activate(place, own_sums, far):
    rows, width = own_sums.shape

    def kernel(place_ref, own_ref, far_ref, out_ref, slope_ref):
        def step(at):
            hidden = own_ref[:, at] + far_ref[:, at].astype(jnp.float32)
            gelu = gelu_value(hidden).astype(jnp.bfloat16)
            for chip in range(4):
                out_ref[chip * rows : (chip + 1) * rows, at] = gelu
            slope_ref[:, at] = gelu_slope(hidden)

        for_tiles(width, step)

    return kernel_call(
        kernel,
        place,
        (own_sums, far),
        [IN_VMEM, IN_VMEM],
        [
            jax.ShapeDtypeStruct((4 * rows, width), jnp.bfloat16),
            jax.ShapeDtypeStruct((rows, width), jnp.float32),
        ],
    )


def chain_slope(place, parts, slope):
    rows, width = slope.shape
    half = rows // len(parts)

    def kernel(place_ref, *refs):
        slope_ref, out_ref = refs[len(parts) :]

        def step(at):
            for i, part in enumerate(refs[: len(parts)]):
                total = part[:half, at].astype(jnp.float32)
                for chip in range(1, 4):
                    total += part[chip * half : (chip + 1) * half, at].astype(jnp.float32)
                here = slice(i * half, (i + 1) * half)
                out_ref[here, at] = (total * slope_ref[here, at]).astype(jnp.bfloat16)

        for_tiles(width, step)

    return kernel_call(kernel, place, (*parts, slope), IN_VMEM, jax.ShapeDtypeStruct((rows, width), jnp.bfloat16))


def features_of(place, raw, kind, pieces):
    rows, depth = raw.shape[2:]
    own = rows // 8

    def kernel(place_ref, raw_ref, out_ref):
        for g in range(0, len(pieces), 8):
            block = [raw_ref[b, kind, p * own : (p + 1) * own] for b, p in pieces[g : g + 8]]
            out_ref[:, g * own : (g + 8) * own] = jnp.concatenate(block).T

    return kernel_call(
        kernel, place, (raw,), IN_VMEM, jax.ShapeDtypeStruct((depth, own * len(pieces)), raw.dtype)
    )


def grad_scratch(tile_shape):
    return [pltpu.VMEM((2, *tile_shape), jnp.float32), pltpu.SemaphoreType.DMA((2,))]


def write_grad(core, parts_of, features, hidden_axis, out_ref, tiles, sems):
    width = parts_of[0][0].shape[1]
    tile = min(TILE, width)
    stores = [None, None]
    step = 0
    for parts, place_of in zip(parts_of, (core, 1 - core)):
        for start in range(0, width, tile):
            units = jnp.concatenate([p[:, start : start + tile] for p in parts])
            total = jnp.dot(features[...], units, preferred_element_type=jnp.float32)
            slot = step % 2
            if stores[slot] is not None:
                stores[slot].wait()
            tiles[slot] = total if hidden_axis == 1 else total.T
            to = pl.ds(pl.multiple_of(place_of * width + start, tile), tile)
            stores[slot] = pltpu.make_async_copy(
                tiles.at[slot], out_ref.at[:, to] if hidden_axis == 1 else out_ref.at[to, :], sems.at[slot]
            )
            stores[slot].start()
            step += 1
    for store in stores:
        store.wait()


def write_input_sums(core, parts_of, w_ref, out_ref, offset):
    rows, width = parts_of[0][0].shape
    own = rows // 16
    dims = (((1,), (1,)), ((), ()))
    for i in range(len(parts_of[0])):
        total = None
        for parts, place_of in zip(parts_of, (core, 1 - core)):
            units = pl.ds(pl.multiple_of(place_of * width, width), width)
            part = lax.dot_general(parts[i][...], w_ref[:, units], dims, preferred_element_type=jnp.float32)
            total = part if total is None else total + part
        total = total.astype(jnp.bfloat16)
        for k in range(16):
            at, block = offset + (k // 4) * own, 4 * i + k % 4
            out_ref[block, at : at + own] = total[k * own : (k + 1) * own]


def input_sums(place, mine, other, weight):
    count = len(mine)
    own = mine[0].shape[0] // 16

    def kernel(place_ref, *refs):
        write_input_sums(place_ref[CORE], (refs[:count], refs[count : 2 * count]), refs[-2], refs[-1], 0)

    out = jax.ShapeDtypeStruct((4 * count, 4 * own, weight.shape[0]), jnp.bfloat16)
    return kernel_call(kernel, place, (*mine, *other, weight), IN_VMEM, out)


def input_sums_and_grad(place, mine, other, weight, kept, features):
    count = len(mine)
    half = count // 2
    blocks, rows, depth = kept.shape
    width = mine[0].shape[1]

    def kernel(place_ref, *refs):
        core = place_ref[CORE]
        parts_of = (refs[:count], refs[count : 2 * count])
        w_ref, kept_ref, features_ref, sums_ref, grad_ref, *scratch = refs[2 * count :]
        sums_ref[:, :rows] = kept_ref[...]
        write_input_sums(core, [parts[half:] for parts in parts_of], w_ref, sums_ref, rows)
        write_grad(core, parts_of, features_ref, 1, grad_ref, *scratch)

    return kernel_call(
        kernel,
        place,
        (*mine, *other, weight, kept, features),
        [IN_VMEM, pl.BlockSpec(memory_space=pl.ANY)],
        [
            jax.ShapeDtypeStruct((blocks, 2 * rows, depth), jnp.bfloat16),
            jax.ShapeDtypeStruct((depth, 2 * width), jnp.float32),
        ],
        grad_scratch((depth, min(TILE, width))),
    )


def weight_grad(place, mine, other, features):
    count = len(mine)
    width = mine[0].shape[1]
    depth = features.shape[0]

    def kernel(place_ref, *refs):
        features_ref, out_ref, *scratch = refs[2 * count :]
        parts_of = (refs[:count], refs[count : 2 * count])
        write_grad(place_ref[CORE], parts_of, features_ref, 0, out_ref, *scratch)

    return kernel_call(
        kernel,
        place,
        (*mine, *other, features),
        pl.BlockSpec(memory_space=pl.ANY),
        jax.ShapeDtypeStruct((2 * width, depth), jnp.float32),
        grad_scratch((min(TILE, width), depth)),
    )


def body(tokens, w_in, w_out, out_grad):
    column, row = lax.axis_index("col"), lax.axis_index("row")
    core, z, y_hi = column % 2, (column // 2) % 4, column // 8
    place = jnp.stack([core, z, y_hi, row]).astype(jnp.int32)
    rows, depth = tokens.shape
    own = rows // 8
    width = w_in.shape[1] // 2
    half = 4 * rows
    quarter = half // 2

    copies = copies_for_row(place, out_grad, tokens)
    raw = lax.all_to_all(copies, "row", 0, 0, tiled=True)
    raw_other = swap(raw, "core")

    w_out_other = swap(lax.dynamic_slice_in_dim(w_out, (1 - core) * width, width, 0), "core")
    w_in_other = swap(lax.dynamic_slice_in_dim(w_in, (1 - core) * width, width, 1), "core")

    def grad_sums(raw, raw_other, chunk):
        return partial_sums(place, raw, raw_other, 0, grad_pieces(4 * chunk), w_out, w_out_other, 0)

    def token_sums(raw, raw_other, chunk):
        return partial_sums(place, raw, raw_other, 1, token_pieces(chunk, 4 * chunk), w_in, w_in_other, 1)

    grad_kept_1, sent_1 = grad_sums(raw, raw_other, 0)
    grad_got_1 = swap(sent_1, "y")
    then = after(sent_1, (raw, raw_other))
    tok_kept, tok_sent = zip(*[token_sums(*then, chunk) for chunk in range(2)])
    tok_got = [swap(sent, order[0]) for sent, order in zip(tok_sent, TOKEN_ORDERS)]
    grad_kept_2, sent_2 = grad_sums(*after(tok_sent, then), 1)
    grad_got_2 = swap(sent_2, "y")

    def z_terms(kept, got):
        parts = b16(f32(kept) + f32(got))
        return lax.all_to_all(parts, "col", 0, 0, axis_index_groups=Z_GROUPS, tiled=True)

    q = quarter // 2
    terms = [z_terms(grad_kept_1, grad_got_1)]
    tok_got = after((grad_got_1, sent_2), tok_got)
    second = [
        swap(b16(f32(k[q:]) + f32(g[q:])), order[1]) for k, g, order in zip(tok_kept, tok_got, TOKEN_ORDERS)
    ]
    second = after((grad_got_2, terms[0]), second)
    own_sums, to_send = fold(place, tok_kept, tok_got, second)
    far = swap(to_send, "y")
    terms.append(z_terms(grad_kept_2, grad_got_2))
    q = quarter // 4

    keep_pieces = token_pieces(0, 0)[:16] + token_pieces(1, 4)[:16]
    first_pieces = token_pieces(0, 0)[16:] + token_pieces(1, 4)[16:]
    grad_order = [(r, 4 * y + z) for y in range(2) for z in range(4) for r in range(8)]
    raw = after(to_send, raw)
    tok_features = features_of(place, raw, 1, keep_pieces + first_pieces)
    grad_features = features_of(place, raw, 0, grad_order)
    far = after((tok_features, grad_features), far)

    spread, slope = activate(place, own_sums, far)
    gelu_keep = lax.all_to_all(spread, "col", 0, 0, axis_index_groups=Z_GROUPS, tiled=True)
    pre_share = chain_slope(place, terms, slope)
    far = swap(pre_share, "y")
    two = [jnp.concatenate([pre_share[i : i + q], far[i : i + q]]) for i in (0, q)]

    gelu_keep, two = lax.optimization_barrier((gelu_keep, two))
    cuts = (0, quarter // 2, 11 * quarter // 8)
    gelu_far = [swap(gelu_keep[: cuts[1]], "y")]
    pre_keep = [jnp.concatenate([t, swap(t, order[1])]) for t, order in zip(two, TOKEN_ORDERS)]

    gelu_far[0], pre_keep, gelu_keep = lax.optimization_barrier((gelu_far[0], pre_keep, gelu_keep))
    gelu_far.append(swap(gelu_keep[cuts[1] : cuts[2]], "y"))
    pre_first = [swap(k, order[0]) for k, order in zip(pre_keep, TOKEN_ORDERS)]
    pre_keep_other = [swap(k, "core") for k in pre_keep]
    kept = input_sums(place, pre_keep, pre_keep_other, w_in)

    gelu_far[1], pre_first, kept, gelu_keep = lax.optimization_barrier((gelu_far[1], pre_first, kept, gelu_keep))
    gelu_far.append(swap(gelu_keep[cuts[2] :], "y"))
    pre_first_other = [swap(f, "core") for f in pre_first]
    sums, w_in_grad = input_sums_and_grad(
        place,
        (*pre_keep, *pre_first),
        (*pre_keep_other, *pre_first_other),
        w_in,
        kept,
        tok_features,
    )
    parts = lax.all_to_all(sums, "row", 0, 0, tiled=True)
    gelu_far[2] = after(sums, gelu_far[2])
    gelu_mine = (gelu_keep, *gelu_far)
    gelu_other = [swap(g, "core") for g in gelu_mine]
    w_out_grad = weight_grad(place, gelu_mine, gelu_other, grad_features)
    parts = after(w_out_grad, parts)
    in_grad = input_total(place, parts)
    return (in_grad, w_in_grad, w_out_grad)


def solution(mesh):
    in_specs = (P("row", "col"), P("col", "row"), P("row", "col"), P("row", "col"))
    out_specs = (P("row", "col"), P("col", "row"), P("row", "col"))
    return jax.shard_map(body, mesh=mesh, in_specs=in_specs, out_specs=out_specs, check_vma=False)
```

```python
import jax
import jax.numpy as jnp
from jax import lax
from jax.experimental import pallas as pl
from jax.experimental.pallas import tpu as pltpu
from jax.sharding import PartitionSpec as P

inv_root_two = 0.7071067811865476
inv_root_two_pi = 0.3989422804014327
AXES = ("row", "col")


def gelu_value(values):
    return 0.5 * values * (1.0 + jax.scipy.special.erf(values * inv_root_two))


def gelu_slope(values):
    return (
        0.5 * (1.0 + jax.scipy.special.erf(values * inv_root_two))
        + values * jnp.exp(-0.5 * values * values) * inv_root_two_pi
    )


def device_index(x, y, z, core):
    return (x * 2 + y % 2) * 16 + (y // 2) * 8 + z * 2 + core


def flip_pairs(x_flip=0, y_flip=0, z_flip=0, core_flip=0):
    return [
        (
            device_index(x, y, z, core),
            device_index(x ^ x_flip, y ^ y_flip, z ^ z_flip, core ^ core_flip),
        )
        for x in range(4)
        for y in range(4)
        for z in range(4)
        for core in range(2)
    ]


FLIPS = {
    "a": flip_pairs(z_flip=1),
    "b": flip_pairs(z_flip=3),
    "y": flip_pairs(y_flip=2),
    "core": flip_pairs(core_flip=1),
    "xa": flip_pairs(x_flip=1),
    "xb": flip_pairs(x_flip=3),
    "yl": flip_pairs(y_flip=1),
}
TOKEN_ORDERS = ("aby", "bay")
GRAD_PARTS = (range(5), range(5, 8))
Z_GROUPS = [[y * 8 + z * 2 + core for z in range(4)] for y in range(2) for core in range(2)]


def swap(values, name):
    return lax.ppermute(values, AXES, FLIPS[name])


def together(*values):
    return lax.optimization_barrier(values)


def f32(values):
    return values.astype(jnp.float32)


def b16(values):
    return values.astype(jnp.bfloat16)


TILE = 512
VMEM_LIMIT = 16 * 1024 * 1024
CORE, Z, Y_HI, ROW = range(4)
IN_VMEM = pl.BlockSpec(memory_space=pltpu.VMEM)


def kernel_call(kernel, place, args, out_specs, out_shape, scratch=()):
    return pl.pallas_call(
        kernel,
        in_specs=[pl.BlockSpec(memory_space=pltpu.SMEM)] + [IN_VMEM] * len(args),
        out_specs=out_specs,
        out_shape=out_shape,
        scratch_shapes=scratch,
        compiler_params=pltpu.CompilerParams(vmem_limit_bytes=VMEM_LIMIT),
    )(place, *args)


def copies_for_row(place, out_grad, tokens):
    rows, depth = tokens.shape
    own = rows // 8

    def kernel(place_ref, grad_ref, tok_ref, out_ref):
        z, y_hi = place_ref[Z], place_ref[Y_HI]
        for i in range(8):
            first, second, third = i >> 2, (i >> 1) & 1, i & 1
            grad = grad_ref[(i & 3) * 2 + (y_hi ^ first)]
            tok = tok_ref[(z ^ first ^ (3 * second)) * 2 + (y_hi ^ third)]
            for to in range(8):
                out_ref[to, 0, i * own : (i + 1) * own] = grad
                out_ref[to, 1, i * own : (i + 1) * own] = tok

    pieces = (8, own, depth)
    out = (8, 2, rows, depth)
    return kernel_call(
        kernel,
        place,
        (out_grad.reshape(pieces), tokens.reshape(pieces)),
        IN_VMEM,
        jax.ShapeDtypeStruct(out, tokens.dtype),
    )


def grad_pieces(blocks):
    return [(r, 4 * y + z) for y in range(2) for z in range(4) for r in blocks]


def token_pieces(chunk, block):
    return [
        (block + r, (first * 4 + second * 2 if chunk == 0 else second * 4 + first * 2) + y)
        for first in range(2)
        for second in range(2)
        for y in range(2)
        for r in range(4)
    ]


def partial_sums(place, raws, kind, pieces, weights, hidden_axis, got=None, split=False, earlier=()):
    rows, depth = raws[0].shape[2:]
    own = rows // 8
    total_rows = own * len(pieces)
    half = total_rows // 2 if split else 0
    width = weights[1].shape[hidden_axis]
    tile = min(TILE, width)
    dims = (((1,), (1 - hidden_axis,)), ((), ()))
    outs = 2 if split else 1

    def kernel(place_ref, l_ref, lo_ref, w_ref, wo_ref, *refs):
        out_refs, left = refs[-1 - outs : -1], refs[-1]
        for i, (block, piece) in enumerate(pieces):
            left[i * own : (i + 1) * own, :depth] = l_ref[block, kind, piece * own : (piece + 1) * own]
            left[i * own : (i + 1) * own, depth:] = lo_ref[block, kind, piece * own : (piece + 1) * own]
        for start in range(0, width, tile):
            mine = pl.ds(pl.multiple_of(place_ref[CORE] * width + start, tile), tile)
            if hidden_axis == 1:
                right = jnp.concatenate([w_ref[:, mine], wo_ref[:, start : start + tile]])
            else:
                right = jnp.concatenate([w_ref[mine, :], wo_ref[start : start + tile, :]], axis=1)
            total = lax.dot_general(left[...], right, dims, preferred_element_type=jnp.float32)
            if got is not None:
                total += refs[0][:, start : start + tile].astype(jnp.float32)
            if split:
                out_refs[0][:, start : start + tile] = total[:half].astype(jnp.bfloat16)
            out_refs[-1][:, start : start + tile] = total[half:].astype(jnp.bfloat16)

    shapes = [jax.ShapeDtypeStruct((total_rows - half, width), jnp.bfloat16)]
    if split:
        shapes = [jax.ShapeDtypeStruct((half, width), jnp.bfloat16)] + shapes
    result = kernel_call(
        kernel,
        place,
        (*raws, *weights) + (() if got is None else (got,)) + tuple(earlier),
        [IN_VMEM] * outs,
        shapes,
        [pltpu.VMEM((total_rows, 2 * depth), jnp.bfloat16)],
    )
    return result if split else result[0]


def input_total(place, parts):
    count, rows, depth = parts.shape
    own = rows // 8

    def kernel(place_ref, parts_ref, out_ref):
        z, y_hi = place_ref[Z], place_ref[Y_HI]
        swapped = place_ref[ROW] >= 4
        for i in range(8):
            first, second, y = i >> 2, (i >> 1) & 1, i & 1
            total = parts_ref[0, i * own : (i + 1) * own].astype(jnp.float32)
            for device in range(1, count):
                total += parts_ref[device, i * own : (i + 1) * own].astype(jnp.float32)
            a = jnp.where(swapped, second, first)
            b = jnp.where(swapped, first, second)
            out_ref[(z ^ a ^ (3 * b)) * 2 + (y_hi ^ y)] = total.astype(jnp.bfloat16)

    out = jax.ShapeDtypeStruct((8, own, depth), jnp.bfloat16)
    return kernel_call(kernel, place, (parts,), IN_VMEM, out).reshape(8 * own, depth)


def for_tiles(width, step):
    tile = min(128, width)

    @pl.loop(0, width // tile)
    def _(i):
        step(pl.ds(pl.multiple_of(i * tile, tile), tile))


def fold(place, held, second):
    count = len(held)
    rows, width = held[0].shape
    half = rows // 2

    def kernel(place_ref, *refs):
        own_ref, send_ref = refs[2 * count :]

        def step(at):
            for i in range(count):
                total = refs[i][:, at].astype(jnp.float32) + refs[count + i][:, at].astype(jnp.float32)
                own_ref[i * half : (i + 1) * half, at] = total[:half]
                send_ref[i * half : (i + 1) * half, at] = total[half:].astype(jnp.bfloat16)

        for_tiles(width, step)

    out = (count * half, width)
    return kernel_call(
        kernel,
        place,
        (*held, *second),
        [IN_VMEM, IN_VMEM],
        [jax.ShapeDtypeStruct(out, jnp.float32), jax.ShapeDtypeStruct(out, jnp.bfloat16)],
    )


def activate(place, own_sums, far):
    shape = jax.ShapeDtypeStruct(own_sums.shape, jnp.bfloat16)

    def kernel(place_ref, own_ref, far_ref, gelu_ref, slope_ref):
        def step(at):
            hidden = own_ref[:, at] + far_ref[:, at].astype(jnp.float32)
            gelu_ref[:, at] = gelu_value(hidden).astype(jnp.bfloat16)
            slope_ref[:, at] = gelu_slope(hidden).astype(jnp.bfloat16)

        for_tiles(shape.shape[1], step)

    return kernel_call(kernel, place, (own_sums, far), [IN_VMEM, IN_VMEM], [shape, shape])


def chain_slope(place, parts, slope, earlier):
    rows, width = slope.shape

    def kernel(place_ref, *refs):
        slope_ref, out_ref = refs[len(parts)], refs[-1]

        def step(at):
            start = 0
            for part in refs[: len(parts)]:
                size = part.shape[0] // 4
                total = part[:size, at].astype(jnp.float32)
                for chip in range(1, 4):
                    total += part[chip * size : (chip + 1) * size, at].astype(jnp.float32)
                here = slice(start, start + size)
                out_ref[here, at] = (total * slope_ref[here, at].astype(jnp.float32)).astype(jnp.bfloat16)
                start += size

        for_tiles(width, step)

    return kernel_call(kernel, place, (*parts, slope, *earlier), IN_VMEM, jax.ShapeDtypeStruct((rows, width), jnp.bfloat16))


def features_of(place, raw, kind, pieces):
    rows, depth = raw.shape[2:]
    own = rows // 8

    def kernel(place_ref, raw_ref, out_ref):
        def rows_of(block, piece):
            if isinstance(piece, tuple):
                y, flip = piece
                piece = 4 * y + (place_ref[Z] ^ flip)
                return raw_ref[block, kind, pl.ds(pl.multiple_of(piece * own, own), own)]
            return raw_ref[block, kind, piece * own : (piece + 1) * own]

        for g in range(0, len(pieces), 8):
            block = [rows_of(*at) for at in pieces[g : g + 8]]
            out_ref[:, g * own : (g + 8) * own] = jnp.concatenate(block).T

    return kernel_call(
        kernel, place, (raw,), IN_VMEM, jax.ShapeDtypeStruct((depth, own * len(pieces)), raw.dtype)
    )


def grad_scratch(depth, width, hidden_axis):
    tile = min(TILE, width)
    steps = 2 * width // tile
    tile_shape = (depth, tile) if hidden_axis == 1 else (tile, depth)
    return [pltpu.VMEM((steps, *tile_shape), jnp.float32), pltpu.SemaphoreType.DMA((steps,))]


def write_grad(core, parts_of, features, hidden_axis, out_ref, tiles, sems):
    width = parts_of[0][0].shape[1]
    tile = min(TILE, width)
    stores = []
    for parts, place_of in zip(parts_of, (core, 1 - core)):
        for start in range(0, width, tile):
            units = jnp.concatenate([p[:, start : start + tile] for p in parts])
            total = jnp.dot(features[...], units, preferred_element_type=jnp.float32)
            step = len(stores)
            tiles[step] = total if hidden_axis == 1 else total.T
            to = pl.ds(pl.multiple_of(place_of * width + start, tile), tile)
            stores.append(
                pltpu.make_async_copy(
                    tiles.at[step], out_ref.at[:, to] if hidden_axis == 1 else out_ref.at[to, :], sems.at[step]
                )
            )
            stores[step].start()
    for store in stores:
        store.wait()


def write_input_sums(core, parts_of, w_ref, out_ref, offset):
    rows, width = parts_of[0][0].shape
    own = rows // 16
    dims = (((1,), (1,)), ((), ()))
    for i in range(len(parts_of[0])):
        total = None
        for parts, place_of in zip(parts_of, (core, 1 - core)):
            units = pl.ds(pl.multiple_of(place_of * width, width), width)
            part = lax.dot_general(parts[i][...], w_ref[:, units], dims, preferred_element_type=jnp.float32)
            total = part if total is None else total + part
        total = total.astype(jnp.bfloat16)
        for k in range(16):
            at, block = offset + (k // 4) * own, 4 * i + k % 4
            out_ref[block, at : at + own] = total[k * own : (k + 1) * own]


def input_sums(place, mine, other, weight):
    count = len(mine)
    own = mine[0].shape[0] // 16

    def kernel(place_ref, *refs):
        write_input_sums(place_ref[CORE], (refs[:count], refs[count : 2 * count]), refs[-2], refs[-1], 0)

    out = jax.ShapeDtypeStruct((4 * count, 4 * own, weight.shape[0]), jnp.bfloat16)
    return kernel_call(kernel, place, (*mine, *other, weight), IN_VMEM, out)


def input_sums_and_grad(place, mine, other, weight, kept, features):
    count = len(mine)
    half = count // 2
    blocks, rows, depth = kept.shape
    width = mine[0].shape[1]

    def kernel(place_ref, *refs):
        core = place_ref[CORE]
        parts_of = (refs[:count], refs[count : 2 * count])
        w_ref, kept_ref, features_ref, sums_ref, grad_ref, *scratch = refs[2 * count :]
        sums_ref[:, :rows] = kept_ref[...]
        write_input_sums(core, [parts[half:] for parts in parts_of], w_ref, sums_ref, rows)
        write_grad(core, parts_of, features_ref, 1, grad_ref, *scratch)

    return kernel_call(
        kernel,
        place,
        (*mine, *other, weight, kept, features),
        [IN_VMEM, pl.BlockSpec(memory_space=pl.ANY)],
        [
            jax.ShapeDtypeStruct((blocks, 2 * rows, depth), jnp.bfloat16),
            jax.ShapeDtypeStruct((depth, 2 * width), jnp.float32),
        ],
        grad_scratch(depth, width, 1),
    )


def weight_grad(place, mine, other, features):
    count = len(mine)
    width = mine[0].shape[1]
    depth = features.shape[0]

    def kernel(place_ref, *refs):
        features_ref, out_ref, *scratch = refs[2 * count :]
        parts_of = (refs[:count], refs[count : 2 * count])
        write_grad(place_ref[CORE], parts_of, features_ref, 0, out_ref, *scratch)

    return kernel_call(
        kernel,
        place,
        (*mine, *other, features),
        pl.BlockSpec(memory_space=pl.ANY),
        jax.ShapeDtypeStruct((2 * width, depth), jnp.float32),
        grad_scratch(depth, width, 0),
    )


def body(tokens, w_in, w_out, out_grad):
    column, row = lax.axis_index("col"), lax.axis_index("row")
    core, z, y_hi = column % 2, (column // 2) % 4, column // 8
    place = jnp.stack([core, z, y_hi, row]).astype(jnp.int32)
    rows, depth = tokens.shape
    own = rows // 8
    width = w_in.shape[1] // 2
    half = 4 * rows
    quarter = half // 2

    copies = copies_for_row(place, out_grad, tokens)
    raw = lax.all_to_all(copies, "row", 0, 0, tiled=True)

    w_out_other = swap(lax.dynamic_slice_in_dim(w_out, (1 - core) * width, width, 0), "core")
    w_in_other = swap(lax.dynamic_slice_in_dim(w_in, (1 - core) * width, width, 1), "core")
    raw, w_out_other, w_in_other = together(raw, w_out_other, w_in_other)
    raw_other = swap(raw, "core")

    raws = (raw, raw_other)

    pieces = [token_pieces(chunk, 4 * chunk) for chunk in range(2)]
    half_of = [(p[:16], p[16:]) for p in pieces]
    w_in_both, w_out_both = (w_in, w_in_other), (w_out, w_out_other)
    first = []
    for _, far_half in half_of:
        first.append(partial_sums(place, raws, 1, far_half, w_in_both, 1))
    tok_got = [swap(f, order[0]) for f, order in zip(first, TOKEN_ORDERS)]
    grad_half_of, sent, grad_got = [], [first[1]], []
    for blocks in GRAD_PARTS:
        pieces = grad_pieces(blocks)
        grad_half_of.append(pieces[: len(pieces) // 2])
        far_half = pieces[len(pieces) // 2 :]
        sent.append(partial_sums(place, raws, 0, far_half, w_out_both, 0))
        grad_got.append(swap(sent[-1], "y"))

    keep_pieces = token_pieces(0, 0)[:16] + token_pieces(1, 4)[:16]
    first_pieces = token_pieces(0, 0)[16:] + token_pieces(1, 4)[16:]
    tok_features = features_of(place, raw, 1, keep_pieces + first_pieces)
    flips = {"a": 1, "b": 3}
    grad_order = [
        (4 * chunk + r, (y, (flips[order[0]] * late) ^ (flips[order[1]] * early)))
        for y in range(2)
        for chunk, order in enumerate(TOKEN_ORDERS)
        for late in range(2)
        for early in range(2)
        for r in range(4)
    ]
    grad_features = features_of(place, raw, 0, grad_order)

    held, sent = [], []
    for (near_half, _), got in zip(half_of, tok_got):
        hold, send = partial_sums(place, raws, 1, near_half, w_in_both, 1, got, split=True, earlier=sent or (tok_features, grad_features))
        held.append(hold)
        sent.append(send)
    second = [swap(s, order[1]) for s, order in zip(sent, TOKEN_ORDERS)]
    terms, earlier = [], sent[1:]
    for near_half, got in zip(grad_half_of, grad_got):
        sums = partial_sums(place, raws, 0, near_half, w_out_both, 0, got, earlier=earlier)
        earlier = ()
        terms.append(lax.all_to_all(sums, "col", 0, 0, axis_index_groups=Z_GROUPS, tiled=True))
    own_sums, to_send = fold(place, held, second)
    far = swap(to_send, "y")
    q = quarter // 4

    gelu_share, slope = activate(place, own_sums, far)
    gelu_near = []
    for start, order in zip((0, q), TOKEN_ORDERS):
        two = jnp.concatenate([gelu_share[start : start + q], swap(gelu_share[start : start + q], order[1])])
        gelu_near += [two, swap(two, order[0])]
    gelu_keep = jnp.concatenate(gelu_near)
    pre_share = chain_slope(place, terms, slope, ())
    far = swap(pre_share, "y")
    two = [jnp.concatenate([pre_share[i : i + q], far[i : i + q]]) for i in (0, q)]

    gelu_keep, two = lax.optimization_barrier((gelu_keep, two))
    cuts = (0, quarter // 4, 11 * quarter // 8)
    gelu_far = [swap(gelu_keep[: cuts[1]], "y")]
    pre_keep = [jnp.concatenate([t, swap(t, order[1])]) for t, order in zip(two, TOKEN_ORDERS)]

    gelu_far[0], pre_keep, gelu_keep = lax.optimization_barrier((gelu_far[0], pre_keep, gelu_keep))
    gelu_far.append(swap(gelu_keep[cuts[1] : cuts[2]], "y"))
    pre_first = [swap(k, order[0]) for k, order in zip(pre_keep, TOKEN_ORDERS)]
    pre_keep_other = [swap(k, "core") for k in pre_keep]
    kept = input_sums(place, pre_keep, pre_keep_other, w_in)

    gelu_far[1], pre_first, kept, gelu_keep = lax.optimization_barrier((gelu_far[1], pre_first, kept, gelu_keep))
    gelu_far.append(swap(gelu_keep[cuts[2] :], "y"))
    pre_first_other = [swap(f, "core") for f in pre_first]
    sums, w_in_grad = input_sums_and_grad(
        place,
        (*pre_keep, *pre_first),
        (*pre_keep_other, *pre_first_other),
        w_in,
        kept,
        tok_features,
    )
    parts = lax.all_to_all(sums, "row", 0, 0, tiled=True)
    w_in_grad, gelu_far[2] = together(w_in_grad, gelu_far[2])
    gelu_mine = (gelu_keep, *gelu_far)
    gelu_other = [swap(g, "core") for g in gelu_mine]
    w_out_grad = weight_grad(place, gelu_mine, gelu_other, grad_features)
    w_out_grad, parts = together(w_out_grad, parts)
    in_grad = input_total(place, parts)
    return (in_grad, w_in_grad, w_out_grad)


def solution(mesh):
    in_specs = (P("row", "col"), P("col", "row"), P("row", "col"), P("row", "col"))
    out_specs = (P("row", "col"), P("col", "row"), P("row", "col"))
    return jax.shard_map(body, mesh=mesh, in_specs=in_specs, out_specs=out_specs, check_vma=False)
```

```python
import jax
import jax.numpy as jnp
from jax import lax
from jax.experimental import pallas as pl
from jax.experimental.pallas import tpu as pltpu
from jax.sharding import PartitionSpec as P

inv_root_two = 0.7071067811865476
inv_root_two_pi = 0.3989422804014327
AXES = ("row", "col")


def gelu_value(values):
    return 0.5 * values * (1.0 + jax.scipy.special.erf(values * inv_root_two))


def gelu_slope(values):
    return (
        0.5 * (1.0 + jax.scipy.special.erf(values * inv_root_two))
        + values * jnp.exp(-0.5 * values * values) * inv_root_two_pi
    )


def device_index(x, y, z, core):
    return (x * 2 + y % 2) * 16 + (y // 2) * 8 + z * 2 + core


def flip_pairs(x_flip=0, y_flip=0, z_flip=0, core_flip=0):
    return [
        (
            device_index(x, y, z, core),
            device_index(x ^ x_flip, y ^ y_flip, z ^ z_flip, core ^ core_flip),
        )
        for x in range(4)
        for y in range(4)
        for z in range(4)
        for core in range(2)
    ]


FLIPS = {
    "a": flip_pairs(z_flip=1),
    "b": flip_pairs(z_flip=3),
    "y": flip_pairs(y_flip=2),
    "core": flip_pairs(core_flip=1),
    "xa": flip_pairs(x_flip=1),
    "xb": flip_pairs(x_flip=3),
    "yl": flip_pairs(y_flip=1),
}
TOKEN_ORDERS = ("aby", "bay")
GRAD_PARTS = (range(5), range(5, 8))
Z_GROUPS = [[y * 8 + z * 2 + core for z in range(4)] for y in range(2) for core in range(2)]


def swap(values, name):
    return lax.ppermute(values, AXES, FLIPS[name])


def together(*values):
    return lax.optimization_barrier(values)


def f32(values):
    return values.astype(jnp.float32)


def b16(values):
    return values.astype(jnp.bfloat16)


TILE = 512
VMEM_LIMIT = 16 * 1024 * 1024
CORE, Z, Y_HI, ROW = range(4)
IN_VMEM = pl.BlockSpec(memory_space=pltpu.VMEM)


def kernel_call(kernel, place, args, out_specs, out_shape, scratch=()):
    return pl.pallas_call(
        kernel,
        in_specs=[pl.BlockSpec(memory_space=pltpu.SMEM)] + [IN_VMEM] * len(args),
        out_specs=out_specs,
        out_shape=out_shape,
        scratch_shapes=scratch,
        compiler_params=pltpu.CompilerParams(vmem_limit_bytes=VMEM_LIMIT),
    )(place, *args)


def copies_for_row(place, out_grad, tokens):
    rows, depth = tokens.shape
    own = rows // 8

    def kernel(place_ref, grad_ref, tok_ref, out_ref):
        z, y_hi = place_ref[Z], place_ref[Y_HI]
        for i in range(8):
            first, second, third = i >> 2, (i >> 1) & 1, i & 1
            grad = grad_ref[(i & 3) * 2 + (y_hi ^ first)]
            tok = tok_ref[(z ^ first ^ (3 * second)) * 2 + (y_hi ^ third)]
            for to in range(8):
                out_ref[to, 0, i * own : (i + 1) * own] = grad
                out_ref[to, 1, i * own : (i + 1) * own] = tok

    pieces = (8, own, depth)
    out = (8, 2, rows, depth)
    return kernel_call(
        kernel,
        place,
        (out_grad.reshape(pieces), tokens.reshape(pieces)),
        IN_VMEM,
        jax.ShapeDtypeStruct(out, tokens.dtype),
    )


def grad_pieces(blocks):
    return [(r, 4 * y + z) for y in range(2) for z in range(4) for r in blocks]


def token_pieces(chunk, block):
    return [
        (block + r, (first * 4 + second * 2 if chunk == 0 else second * 4 + first * 2) + y)
        for first in range(2)
        for second in range(2)
        for y in range(2)
        for r in range(4)
    ]


def partial_sums(place, raws, kind, pieces, weights, hidden_axis, got=None, split=False, earlier=()):
    rows, depth = raws[0].shape[2:]
    own = rows // 8
    total_rows = own * len(pieces)
    half = total_rows // 2 if split else 0
    width = weights[1].shape[hidden_axis]
    tile = min(TILE, width)
    dims = (((1,), (1 - hidden_axis,)), ((), ()))
    outs = 2 if split else 1

    def kernel(place_ref, l_ref, lo_ref, w_ref, wo_ref, *refs):
        out_refs, left = refs[-1 - outs : -1], refs[-1]
        for i, (block, piece) in enumerate(pieces):
            left[i * own : (i + 1) * own, :depth] = l_ref[block, kind, piece * own : (piece + 1) * own]
            left[i * own : (i + 1) * own, depth:] = lo_ref[block, kind, piece * own : (piece + 1) * own]
        for start in range(0, width, tile):
            mine = pl.ds(pl.multiple_of(place_ref[CORE] * width + start, tile), tile)
            if hidden_axis == 1:
                right = jnp.concatenate([w_ref[:, mine], wo_ref[:, start : start + tile]])
            else:
                right = jnp.concatenate([w_ref[mine, :], wo_ref[start : start + tile, :]], axis=1)
            total = lax.dot_general(left[...], right, dims, preferred_element_type=jnp.float32)
            if got is not None:
                total += refs[0][:, start : start + tile].astype(jnp.float32)
            if split:
                out_refs[0][:, start : start + tile] = total[:half].astype(jnp.bfloat16)
            out_refs[-1][:, start : start + tile] = total[half:].astype(jnp.bfloat16)

    shapes = [jax.ShapeDtypeStruct((total_rows - half, width), jnp.bfloat16)]
    if split:
        shapes = [jax.ShapeDtypeStruct((half, width), jnp.bfloat16)] + shapes
    result = kernel_call(
        kernel,
        place,
        (*raws, *weights) + (() if got is None else (got,)) + tuple(earlier),
        [IN_VMEM] * outs,
        shapes,
        [pltpu.VMEM((total_rows, 2 * depth), jnp.bfloat16)],
    )
    return result if split else result[0]


def input_total(place, parts):
    count, rows, depth = parts.shape
    own = rows // 8

    def kernel(place_ref, parts_ref, out_ref):
        z, y_hi = place_ref[Z], place_ref[Y_HI]
        swapped = place_ref[ROW] >= 4
        for i in range(8):
            first, second, y = i >> 2, (i >> 1) & 1, i & 1
            total = parts_ref[0, i * own : (i + 1) * own].astype(jnp.float32)
            for device in range(1, count):
                total += parts_ref[device, i * own : (i + 1) * own].astype(jnp.float32)
            a = jnp.where(swapped, second, first)
            b = jnp.where(swapped, first, second)
            out_ref[(z ^ a ^ (3 * b)) * 2 + (y_hi ^ y)] = total.astype(jnp.bfloat16)

    out = jax.ShapeDtypeStruct((8, own, depth), jnp.bfloat16)
    return kernel_call(kernel, place, (parts,), IN_VMEM, out).reshape(8 * own, depth)


def for_tiles(width, step):
    tile = min(128, width)

    @pl.loop(0, width // tile)
    def _(i):
        step(pl.ds(pl.multiple_of(i * tile, tile), tile))


def fold(place, held, second, earlier):
    count = len(held)
    rows, width = held[0].shape
    half = rows // 2

    def kernel(place_ref, *refs):
        own_ref, send_ref = refs[-2:]

        def step(at):
            for i in range(count):
                total = refs[i][:, at].astype(jnp.float32) + refs[count + i][:, at].astype(jnp.float32)
                own_ref[i * half : (i + 1) * half, at] = total[:half]
                send_ref[i * half : (i + 1) * half, at] = total[half:].astype(jnp.bfloat16)

        for_tiles(width, step)

    out = (count * half, width)
    return kernel_call(
        kernel,
        place,
        (*held, *second, *earlier),
        [IN_VMEM, IN_VMEM],
        [jax.ShapeDtypeStruct(out, jnp.float32), jax.ShapeDtypeStruct(out, jnp.bfloat16)],
    )


def activate(place, own_sums, far):
    shape = jax.ShapeDtypeStruct(own_sums.shape, jnp.bfloat16)

    def kernel(place_ref, own_ref, far_ref, gelu_ref, slope_ref):
        def step(at):
            hidden = own_ref[:, at] + far_ref[:, at].astype(jnp.float32)
            gelu_ref[:, at] = gelu_value(hidden).astype(jnp.bfloat16)
            slope_ref[:, at] = gelu_slope(hidden).astype(jnp.bfloat16)

        for_tiles(shape.shape[1], step)

    return kernel_call(kernel, place, (own_sums, far), [IN_VMEM, IN_VMEM], [shape, shape])


def chain_slope(place, parts, slope, earlier):
    rows, width = slope.shape

    def kernel(place_ref, *refs):
        slope_ref, out_ref = refs[len(parts)], refs[-1]

        def step(at):
            start = 0
            for part in refs[: len(parts)]:
                size = part.shape[0] // 4
                total = part[:size, at].astype(jnp.float32)
                for chip in range(1, 4):
                    total += part[chip * size : (chip + 1) * size, at].astype(jnp.float32)
                here = slice(start, start + size)
                out_ref[here, at] = (total * slope_ref[here, at].astype(jnp.float32)).astype(jnp.bfloat16)
                start += size

        for_tiles(width, step)

    return kernel_call(kernel, place, (*parts, slope, *earlier), IN_VMEM, jax.ShapeDtypeStruct((rows, width), jnp.bfloat16))


def features_of(place, raw, kind, pieces):
    rows, depth = raw.shape[2:]
    own = rows // 8

    def kernel(place_ref, raw_ref, out_ref):
        def rows_of(block, piece):
            if isinstance(piece, tuple):
                y, flip = piece
                piece = 4 * y + (place_ref[Z] ^ flip)
                return raw_ref[block, kind, pl.ds(pl.multiple_of(piece * own, own), own)]
            return raw_ref[block, kind, piece * own : (piece + 1) * own]

        for g in range(0, len(pieces), 8):
            block = [rows_of(*at) for at in pieces[g : g + 8]]
            out_ref[:, g * own : (g + 8) * own] = jnp.concatenate(block).T

    return kernel_call(
        kernel, place, (raw,), IN_VMEM, jax.ShapeDtypeStruct((depth, own * len(pieces)), raw.dtype)
    )


def grad_scratch(depth, width, hidden_axis):
    tile = min(TILE, width)
    steps = 2 * width // tile
    tile_shape = (depth, tile) if hidden_axis == 1 else (tile, depth)
    return [pltpu.VMEM((steps, *tile_shape), jnp.float32), pltpu.SemaphoreType.DMA((steps,))]


def write_grad(core, parts_of, features, hidden_axis, out_ref, tiles, sems):
    width = parts_of[0][0].shape[1]
    tile = min(TILE, width)
    stores = []
    for parts, place_of in zip(parts_of, (core, 1 - core)):
        for start in range(0, width, tile):
            units = jnp.concatenate([p[:, start : start + tile] for p in parts])
            total = jnp.dot(features[...], units, preferred_element_type=jnp.float32)
            step = len(stores)
            tiles[step] = total if hidden_axis == 1 else total.T
            to = pl.ds(pl.multiple_of(place_of * width + start, tile), tile)
            stores.append(
                pltpu.make_async_copy(
                    tiles.at[step], out_ref.at[:, to] if hidden_axis == 1 else out_ref.at[to, :], sems.at[step]
                )
            )
            stores[step].start()
    for store in stores:
        store.wait()


def write_input_sums(core, parts_of, w_ref, out_ref, offset):
    rows, width = parts_of[0][0].shape
    own = rows // 16
    dims = (((1,), (1,)), ((), ()))
    for i in range(len(parts_of[0])):
        total = None
        for parts, place_of in zip(parts_of, (core, 1 - core)):
            units = pl.ds(pl.multiple_of(place_of * width, width), width)
            part = lax.dot_general(parts[i][...], w_ref[:, units], dims, preferred_element_type=jnp.float32)
            total = part if total is None else total + part
        total = total.astype(jnp.bfloat16)
        for k in range(16):
            at, block = offset + (k // 4) * own, 4 * i + k % 4
            out_ref[block, at : at + own] = total[k * own : (k + 1) * own]


def input_sums(place, mine, other, weight):
    count = len(mine)
    own = mine[0].shape[0] // 16

    def kernel(place_ref, *refs):
        write_input_sums(place_ref[CORE], (refs[:count], refs[count : 2 * count]), refs[-2], refs[-1], 0)

    out = jax.ShapeDtypeStruct((4 * count, 4 * own, weight.shape[0]), jnp.bfloat16)
    return kernel_call(kernel, place, (*mine, *other, weight), IN_VMEM, out)


def input_sums_and_grad(place, mine, other, weight, kept, features):
    count = len(mine)
    half = count // 2
    blocks, rows, depth = kept.shape
    width = mine[0].shape[1]

    def kernel(place_ref, *refs):
        core = place_ref[CORE]
        parts_of = (refs[:count], refs[count : 2 * count])
        w_ref, kept_ref, features_ref, sums_ref, grad_ref, *scratch = refs[2 * count :]
        sums_ref[:, :rows] = kept_ref[...]
        write_input_sums(core, [parts[half:] for parts in parts_of], w_ref, sums_ref, rows)
        write_grad(core, parts_of, features_ref, 1, grad_ref, *scratch)

    return kernel_call(
        kernel,
        place,
        (*mine, *other, weight, kept, features),
        [IN_VMEM, pl.BlockSpec(memory_space=pl.ANY)],
        [
            jax.ShapeDtypeStruct((blocks, 2 * rows, depth), jnp.bfloat16),
            jax.ShapeDtypeStruct((depth, 2 * width), jnp.float32),
        ],
        grad_scratch(depth, width, 1),
    )


def weight_grad(place, mine, other, features):
    count = len(mine)
    width = mine[0].shape[1]
    depth = features.shape[0]

    def kernel(place_ref, *refs):
        features_ref, out_ref, *scratch = refs[2 * count :]
        parts_of = (refs[:count], refs[count : 2 * count])
        write_grad(place_ref[CORE], parts_of, features_ref, 0, out_ref, *scratch)

    return kernel_call(
        kernel,
        place,
        (*mine, *other, features),
        pl.BlockSpec(memory_space=pl.ANY),
        jax.ShapeDtypeStruct((2 * width, depth), jnp.float32),
        grad_scratch(depth, width, 0),
    )


def body(tokens, w_in, w_out, out_grad):
    column, row = lax.axis_index("col"), lax.axis_index("row")
    core, z, y_hi = column % 2, (column // 2) % 4, column // 8
    place = jnp.stack([core, z, y_hi, row]).astype(jnp.int32)
    rows, depth = tokens.shape
    own = rows // 8
    width = w_in.shape[1] // 2
    half = 4 * rows
    quarter = half // 2

    copies = copies_for_row(place, out_grad, tokens)
    raw = lax.all_to_all(copies, "row", 0, 0, tiled=True)

    w_out_other = swap(lax.dynamic_slice_in_dim(w_out, (1 - core) * width, width, 0), "core")
    w_in_other = swap(lax.dynamic_slice_in_dim(w_in, (1 - core) * width, width, 1), "core")
    raw, w_out_other, w_in_other = together(raw, w_out_other, w_in_other)
    raw_other = swap(raw, "core")

    raws = (raw, raw_other)

    pieces = [token_pieces(chunk, 4 * chunk) for chunk in range(2)]
    half_of = [(p[:16], p[16:]) for p in pieces]
    w_in_both, w_out_both = (w_in, w_in_other), (w_out, w_out_other)
    first = []
    for _, far_half in half_of:
        first.append(partial_sums(place, raws, 1, far_half, w_in_both, 1))
    tok_got = [swap(f, order[0]) for f, order in zip(first, TOKEN_ORDERS)]
    grad_half_of, sent, grad_got = [], [first[1]], []
    for blocks in GRAD_PARTS:
        pieces = grad_pieces(blocks)
        grad_half_of.append(pieces[: len(pieces) // 2])
        far_half = pieces[len(pieces) // 2 :]
        sent.append(partial_sums(place, raws, 0, far_half, w_out_both, 0))
        grad_got.append(swap(sent[-1], "y"))

    keep_pieces = token_pieces(0, 0)[:16] + token_pieces(1, 4)[:16]
    first_pieces = token_pieces(0, 0)[16:] + token_pieces(1, 4)[16:]
    tok_features = features_of(place, raw, 1, keep_pieces + first_pieces)
    flips = {"a": 1, "b": 3}
    grad_order = [
        (4 * chunk + r, (y, (flips[order[0]] * late) ^ (flips[order[1]] * early)))
        for y in range(2)
        for chunk, order in enumerate(TOKEN_ORDERS)
        for late in range(2)
        for early in range(2)
        for r in range(4)
    ]
    grad_features = features_of(place, raw, 0, grad_order)

    held, sent = [], []
    for (near_half, _), got in zip(half_of, tok_got):
        hold, send = partial_sums(place, raws, 1, near_half, w_in_both, 1, got, split=True, earlier=sent or (tok_features, grad_features))
        held.append(hold)
        sent.append(send)
    second = [swap(s, order[1]) for s, order in zip(sent, TOKEN_ORDERS)]
    terms, earlier = [], sent[1:]
    for near_half, got in zip(grad_half_of, grad_got):
        sums = partial_sums(place, raws, 0, near_half, w_out_both, 0, got, earlier=earlier)
        earlier = ()
        terms.append(lax.all_to_all(sums, "col", 0, 0, axis_index_groups=Z_GROUPS, tiled=True))
    own_sums, to_send = fold(place, held, second, [sums])
    far = swap(to_send, "y")
    q = quarter // 4

    gelu_share, slope = activate(place, own_sums, far)
    gelu_near = []
    for start, order in zip((0, q), TOKEN_ORDERS):
        two = jnp.concatenate([gelu_share[start : start + q], swap(gelu_share[start : start + q], order[1])])
        gelu_near += [two, swap(two, order[0])]
    gelu_keep = jnp.concatenate(gelu_near)
    pre_share = chain_slope(place, terms, slope, ())
    far = swap(pre_share, "y")
    two = [jnp.concatenate([pre_share[i : i + q], far[i : i + q]]) for i in (0, q)]

    pre_keep = [jnp.concatenate([t, swap(t, order[1])]) for t, order in zip(two, TOKEN_ORDERS)]

    gelu_keep, pre_keep = together(gelu_keep, pre_keep)
    cut = 21 * quarter // 16
    gelu_far = [swap(gelu_keep[:cut], "y")]
    pre_first = [swap(k, order[0]) for k, order in zip(pre_keep, TOKEN_ORDERS)]
    pre_keep_other = [swap(k, "core") for k in pre_keep]
    kept = input_sums(place, pre_keep, pre_keep_other, w_in)

    gelu_far[0], pre_first, kept, gelu_keep = together(gelu_far[0], pre_first, kept, gelu_keep)
    gelu_far.append(swap(gelu_keep[cut:], "y"))
    pre_first_other = [swap(f, "core") for f in pre_first]
    sums, w_in_grad = input_sums_and_grad(
        place,
        (*pre_keep, *pre_first),
        (*pre_keep_other, *pre_first_other),
        w_in,
        kept,
        tok_features,
    )
    parts = lax.all_to_all(sums, "row", 0, 0, tiled=True)
    w_in_grad, gelu_far[1] = together(w_in_grad, gelu_far[1])
    gelu_mine = (gelu_keep, *gelu_far)
    gelu_other = [swap(g, "core") for g in gelu_mine]
    w_out_grad = weight_grad(place, gelu_mine, gelu_other, grad_features)
    w_out_grad, parts = together(w_out_grad, parts)
    in_grad = input_total(place, parts)
    return (in_grad, w_in_grad, w_out_grad)


def solution(mesh):
    in_specs = (P("row", "col"), P("col", "row"), P("row", "col"), P("row", "col"))
    out_specs = (P("row", "col"), P("col", "row"), P("row", "col"))
    return jax.shard_map(body, mesh=mesh, in_specs=in_specs, out_specs=out_specs, check_vma=False)
```

```python
import jax
import jax.numpy as jnp
from jax import lax
from jax.experimental import pallas as pl
from jax.experimental.pallas import tpu as pltpu
from jax.sharding import PartitionSpec as P

inv_root_two = 0.7071067811865476
inv_root_two_pi = 0.3989422804014327
AXES = ("row", "col")


def gelu_value(values):
    return 0.5 * values * (1.0 + jax.scipy.special.erf(values * inv_root_two))


def gelu_slope(values):
    return (
        0.5 * (1.0 + jax.scipy.special.erf(values * inv_root_two))
        + values * jnp.exp(-0.5 * values * values) * inv_root_two_pi
    )


def device_index(x, y, z, core):
    return (x * 2 + y % 2) * 16 + (y // 2) * 8 + z * 2 + core


def flip_pairs(x_flip=0, y_flip=0, z_flip=0, core_flip=0):
    return [
        (
            device_index(x, y, z, core),
            device_index(x ^ x_flip, y ^ y_flip, z ^ z_flip, core ^ core_flip),
        )
        for x in range(4)
        for y in range(4)
        for z in range(4)
        for core in range(2)
    ]


FLIPS = {
    "a": flip_pairs(z_flip=1),
    "b": flip_pairs(z_flip=3),
    "y": flip_pairs(y_flip=2),
    "core": flip_pairs(core_flip=1),
    "xa": flip_pairs(x_flip=1),
    "xb": flip_pairs(x_flip=3),
    "yl": flip_pairs(y_flip=1),
}
TOKEN_ORDERS = ("aby", "bay")
GRAD_PARTS = (range(5), range(5, 8))
Z_GROUPS = [[y * 8 + z * 2 + core for z in range(4)] for y in range(2) for core in range(2)]


def swap(values, name):
    return lax.ppermute(values, AXES, FLIPS[name])


def together(*values):
    return lax.optimization_barrier(values)


def f32(values):
    return values.astype(jnp.float32)


def b16(values):
    return values.astype(jnp.bfloat16)


TILE = 512
VMEM_LIMIT = 16 * 1024 * 1024
CORE, Z, Y_HI, ROW = range(4)
IN_VMEM = pl.BlockSpec(memory_space=pltpu.VMEM)


def kernel_call(kernel, place, args, out_specs, out_shape, scratch=()):
    return pl.pallas_call(
        kernel,
        in_specs=[pl.BlockSpec(memory_space=pltpu.SMEM)] + [IN_VMEM] * len(args),
        out_specs=out_specs,
        out_shape=out_shape,
        scratch_shapes=scratch,
        compiler_params=pltpu.CompilerParams(vmem_limit_bytes=VMEM_LIMIT),
    )(place, *args)


def copies_for_row(place, out_grad, tokens):
    rows, depth = tokens.shape
    own = rows // 8

    def kernel(place_ref, grad_ref, tok_ref, out_ref):
        z, y_hi = place_ref[Z], place_ref[Y_HI]
        for i in range(8):
            first, second, third = i >> 2, (i >> 1) & 1, i & 1
            grad = grad_ref[(i & 3) * 2 + (y_hi ^ first)]
            tok = tok_ref[(z ^ first ^ (3 * second)) * 2 + (y_hi ^ third)]
            for to in range(8):
                out_ref[to, 0, i * own : (i + 1) * own] = grad
                out_ref[to, 1, i * own : (i + 1) * own] = tok

    pieces = (8, own, depth)
    out = (8, 2, rows, depth)
    return kernel_call(
        kernel,
        place,
        (out_grad.reshape(pieces), tokens.reshape(pieces)),
        IN_VMEM,
        jax.ShapeDtypeStruct(out, tokens.dtype),
    )


def grad_pieces(blocks):
    return [(r, 4 * y + z) for y in range(2) for z in range(4) for r in blocks]


def token_pieces(chunk, block):
    return [
        (block + r, (first * 4 + second * 2 if chunk == 0 else second * 4 + first * 2) + y)
        for first in range(2)
        for second in range(2)
        for y in range(2)
        for r in range(4)
    ]


def partial_sums(place, raws, kind, pieces, weights, hidden_axis, got=None, split=False, earlier=()):
    rows, depth = raws[0].shape[2:]
    own = rows // 8
    total_rows = own * len(pieces)
    half = total_rows // 2 if split else 0
    width = weights[1].shape[hidden_axis]
    tile = min(TILE, width)
    dims = (((1,), (1 - hidden_axis,)), ((), ()))
    outs = 2 if split else 1

    def kernel(place_ref, l_ref, lo_ref, w_ref, wo_ref, *refs):
        out_refs, left = refs[-1 - outs : -1], refs[-1]
        for i, (block, piece) in enumerate(pieces):
            left[i * own : (i + 1) * own, :depth] = l_ref[block, kind, piece * own : (piece + 1) * own]
            left[i * own : (i + 1) * own, depth:] = lo_ref[block, kind, piece * own : (piece + 1) * own]
        for start in range(0, width, tile):
            mine = pl.ds(pl.multiple_of(place_ref[CORE] * width + start, tile), tile)
            if hidden_axis == 1:
                right = jnp.concatenate([w_ref[:, mine], wo_ref[:, start : start + tile]])
            else:
                right = jnp.concatenate([w_ref[mine, :], wo_ref[start : start + tile, :]], axis=1)
            total = lax.dot_general(left[...], right, dims, preferred_element_type=jnp.float32)
            if got is not None:
                total += refs[0][:, start : start + tile].astype(jnp.float32)
            if split:
                out_refs[0][:, start : start + tile] = total[:half].astype(jnp.bfloat16)
            out_refs[-1][:, start : start + tile] = total[half:].astype(jnp.bfloat16)

    shapes = [jax.ShapeDtypeStruct((total_rows - half, width), jnp.bfloat16)]
    if split:
        shapes = [jax.ShapeDtypeStruct((half, width), jnp.bfloat16)] + shapes
    result = kernel_call(
        kernel,
        place,
        (*raws, *weights) + (() if got is None else (got,)) + tuple(earlier),
        [IN_VMEM] * outs,
        shapes,
        [pltpu.VMEM((total_rows, 2 * depth), jnp.bfloat16)],
    )
    return result if split else result[0]


def input_total(place, parts):
    count, rows, depth = parts.shape
    own = rows // 8

    def kernel(place_ref, parts_ref, out_ref):
        z, y_hi = place_ref[Z], place_ref[Y_HI]
        swapped = place_ref[ROW] >= 4
        for i in range(8):
            first, second, y = i >> 2, (i >> 1) & 1, i & 1
            total = parts_ref[0, i * own : (i + 1) * own].astype(jnp.float32)
            for device in range(1, count):
                total += parts_ref[device, i * own : (i + 1) * own].astype(jnp.float32)
            a = jnp.where(swapped, second, first)
            b = jnp.where(swapped, first, second)
            out_ref[(z ^ a ^ (3 * b)) * 2 + (y_hi ^ y)] = total.astype(jnp.bfloat16)

    out = jax.ShapeDtypeStruct((8, own, depth), jnp.bfloat16)
    return kernel_call(kernel, place, (parts,), IN_VMEM, out).reshape(8 * own, depth)


def for_tiles(width, step):
    tile = min(128, width)

    @pl.loop(0, width // tile)
    def _(i):
        step(pl.ds(pl.multiple_of(i * tile, tile), tile))


def fold(place, held, second, earlier):
    count = len(held)
    rows, width = held[0].shape
    half = rows // 2

    def kernel(place_ref, *refs):
        own_ref, send_ref = refs[-2:]

        def step(at):
            for i in range(count):
                total = refs[i][:, at].astype(jnp.float32) + refs[count + i][:, at].astype(jnp.float32)
                own_ref[i * half : (i + 1) * half, at] = total[:half]
                send_ref[i * half : (i + 1) * half, at] = total[half:].astype(jnp.bfloat16)

        for_tiles(width, step)

    out = (count * half, width)
    return kernel_call(
        kernel,
        place,
        (*held, *second, *earlier),
        [IN_VMEM, IN_VMEM],
        [jax.ShapeDtypeStruct(out, jnp.float32), jax.ShapeDtypeStruct(out, jnp.bfloat16)],
    )


def activate(place, own_sums, far):
    shape = jax.ShapeDtypeStruct(own_sums.shape, jnp.bfloat16)

    def kernel(place_ref, own_ref, far_ref, gelu_ref, slope_ref):
        def step(at):
            hidden = own_ref[:, at] + far_ref[:, at].astype(jnp.float32)
            gelu_ref[:, at] = gelu_value(hidden).astype(jnp.bfloat16)
            slope_ref[:, at] = gelu_slope(hidden).astype(jnp.bfloat16)

        for_tiles(shape.shape[1], step)

    return kernel_call(kernel, place, (own_sums, far), [IN_VMEM, IN_VMEM], [shape, shape])


def chain_slope(place, parts, slope, earlier):
    rows, width = slope.shape

    def kernel(place_ref, *refs):
        slope_ref, out_ref = refs[len(parts)], refs[-1]

        def step(at):
            start = 0
            for part in refs[: len(parts)]:
                size = part.shape[0] // 4
                total = part[:size, at].astype(jnp.float32)
                for chip in range(1, 4):
                    total += part[chip * size : (chip + 1) * size, at].astype(jnp.float32)
                here = slice(start, start + size)
                out_ref[here, at] = (total * slope_ref[here, at].astype(jnp.float32)).astype(jnp.bfloat16)
                start += size

        for_tiles(width, step)

    return kernel_call(kernel, place, (*parts, slope, *earlier), IN_VMEM, jax.ShapeDtypeStruct((rows, width), jnp.bfloat16))


def features_of(place, raw, kind, pieces):
    rows, depth = raw.shape[2:]
    own = rows // 8

    def kernel(place_ref, raw_ref, out_ref):
        def rows_of(block, piece):
            if isinstance(piece, tuple):
                y, flip = piece
                piece = 4 * y + (place_ref[Z] ^ flip)
                return raw_ref[block, kind, pl.ds(pl.multiple_of(piece * own, own), own)]
            return raw_ref[block, kind, piece * own : (piece + 1) * own]

        for g in range(0, len(pieces), 8):
            block = [rows_of(*at) for at in pieces[g : g + 8]]
            out_ref[:, g * own : (g + 8) * own] = jnp.concatenate(block).T

    return kernel_call(
        kernel, place, (raw,), IN_VMEM, jax.ShapeDtypeStruct((depth, own * len(pieces)), raw.dtype)
    )


def grad_scratch(depth, width, hidden_axis):
    tile = min(TILE, width)
    steps = 2 * width // tile
    tile_shape = (depth, tile) if hidden_axis == 1 else (tile, depth)
    return [pltpu.VMEM((steps, *tile_shape), jnp.float32), pltpu.SemaphoreType.DMA((steps,))]


def write_grad(core, parts_of, features, hidden_axis, out_ref, tiles, sems):
    width = parts_of[0][0].shape[1]
    tile = min(TILE, width)
    stores = []
    for parts, place_of in zip(parts_of, (core, 1 - core)):
        for start in range(0, width, tile):
            units = jnp.concatenate([p[:, start : start + tile] for p in parts])
            total = jnp.dot(features[...], units, preferred_element_type=jnp.float32)
            step = len(stores)
            tiles[step] = total if hidden_axis == 1 else total.T
            to = pl.ds(pl.multiple_of(place_of * width + start, tile), tile)
            stores.append(
                pltpu.make_async_copy(
                    tiles.at[step], out_ref.at[:, to] if hidden_axis == 1 else out_ref.at[to, :], sems.at[step]
                )
            )
            stores[step].start()
    for store in stores:
        store.wait()


def write_input_sums(core, parts_of, w_ref, out_ref, offset):
    rows, width = parts_of[0][0].shape
    own = rows // 16
    dims = (((1,), (1,)), ((), ()))
    for i in range(len(parts_of[0])):
        total = None
        for parts, place_of in zip(parts_of, (core, 1 - core)):
            units = pl.ds(pl.multiple_of(place_of * width, width), width)
            part = lax.dot_general(parts[i][...], w_ref[:, units], dims, preferred_element_type=jnp.float32)
            total = part if total is None else total + part
        total = total.astype(jnp.bfloat16)
        for k in range(16):
            at, block = offset + (k // 4) * own, 4 * i + k % 4
            out_ref[block, at : at + own] = total[k * own : (k + 1) * own]


def input_sums(place, mine, other, weight):
    count = len(mine)
    own = mine[0].shape[0] // 16

    def kernel(place_ref, *refs):
        write_input_sums(place_ref[CORE], (refs[:count], refs[count : 2 * count]), refs[-2], refs[-1], 0)

    out = jax.ShapeDtypeStruct((4 * count, 4 * own, weight.shape[0]), jnp.bfloat16)
    return kernel_call(kernel, place, (*mine, *other, weight), IN_VMEM, out)


def input_sums_and_grad(place, mine, other, weight, kept, features):
    count = len(mine)
    half = count // 2
    blocks, rows, depth = kept.shape
    width = mine[0].shape[1]

    def kernel(place_ref, *refs):
        core = place_ref[CORE]
        parts_of = (refs[:count], refs[count : 2 * count])
        w_ref, kept_ref, features_ref, sums_ref, grad_ref, *scratch = refs[2 * count :]
        sums_ref[:, :rows] = kept_ref[...]
        write_input_sums(core, [parts[half:] for parts in parts_of], w_ref, sums_ref, rows)
        write_grad(core, parts_of, features_ref, 1, grad_ref, *scratch)

    return kernel_call(
        kernel,
        place,
        (*mine, *other, weight, kept, features),
        [IN_VMEM, pl.BlockSpec(memory_space=pl.ANY)],
        [
            jax.ShapeDtypeStruct((blocks, 2 * rows, depth), jnp.bfloat16),
            jax.ShapeDtypeStruct((depth, 2 * width), jnp.float32),
        ],
        grad_scratch(depth, width, 1),
    )


def weight_grad(place, mine, other, features):
    count = len(mine)
    width = mine[0].shape[1]
    depth = features.shape[0]

    def kernel(place_ref, *refs):
        features_ref, out_ref, *scratch = refs[2 * count :]
        parts_of = (refs[:count], refs[count : 2 * count])
        write_grad(place_ref[CORE], parts_of, features_ref, 0, out_ref, *scratch)

    return kernel_call(
        kernel,
        place,
        (*mine, *other, features),
        pl.BlockSpec(memory_space=pl.ANY),
        jax.ShapeDtypeStruct((2 * width, depth), jnp.float32),
        grad_scratch(depth, width, 0),
    )


def body(tokens, w_in, w_out, out_grad):
    column, row = lax.axis_index("col"), lax.axis_index("row")
    core, z, y_hi = column % 2, (column // 2) % 4, column // 8
    place = jnp.stack([core, z, y_hi, row]).astype(jnp.int32)
    rows, depth = tokens.shape
    own = rows // 8
    width = w_in.shape[1] // 2
    half = 4 * rows
    quarter = half // 2

    copies = copies_for_row(place, out_grad, tokens)
    raw = lax.all_to_all(copies, "row", 0, 0, tiled=True)

    w_out_other = swap(lax.dynamic_slice_in_dim(w_out, (1 - core) * width, width, 0), "core")
    w_in_other = swap(lax.dynamic_slice_in_dim(w_in, (1 - core) * width, width, 1), "core")
    raw, w_out_other, w_in_other = together(raw, w_out_other, w_in_other)
    raw_other = swap(raw, "core")

    raws = (raw, raw_other)

    pieces = [token_pieces(chunk, 4 * chunk) for chunk in range(2)]
    half_of = [(p[:16], p[16:]) for p in pieces]
    w_in_both, w_out_both = (w_in, w_in_other), (w_out, w_out_other)
    first = []
    for _, far_half in half_of:
        first.append(partial_sums(place, raws, 1, far_half, w_in_both, 1))
    tok_got = [swap(f, order[0]) for f, order in zip(first, TOKEN_ORDERS)]
    grad_half_of, sent, grad_got = [], [first[1]], []
    for blocks in GRAD_PARTS:
        pieces = grad_pieces(blocks)
        grad_half_of.append(pieces[: len(pieces) // 2])
        far_half = pieces[len(pieces) // 2 :]
        sent.append(partial_sums(place, raws, 0, far_half, w_out_both, 0))
        grad_got.append(swap(sent[-1], "y"))

    keep_pieces = token_pieces(0, 0)[:16] + token_pieces(1, 4)[:16]
    first_pieces = token_pieces(0, 0)[16:] + token_pieces(1, 4)[16:]
    tok_features = features_of(place, raw, 1, keep_pieces + first_pieces)
    flips = {"a": 1, "b": 3}
    grad_order = [
        (4 * chunk + r, (y, (flips[order[0]] * late) ^ (flips[order[1]] * early)))
        for y in range(2)
        for chunk, order in enumerate(TOKEN_ORDERS)
        for late in range(2)
        for early in range(2)
        for r in range(4)
    ]
    grad_features = features_of(place, raw, 0, grad_order)

    held, sent = [], []
    for (near_half, _), got in zip(half_of, tok_got):
        hold, send = partial_sums(place, raws, 1, near_half, w_in_both, 1, got, split=True, earlier=sent or (tok_features, grad_features))
        held.append(hold)
        sent.append(send)
    second = [swap(s, order[1]) for s, order in zip(sent, TOKEN_ORDERS)]
    terms, earlier = [], sent[1:]
    for near_half, got in zip(grad_half_of, grad_got):
        sums = partial_sums(place, raws, 0, near_half, w_out_both, 0, got, earlier=earlier)
        earlier = ()
        terms.append(lax.all_to_all(sums, "col", 0, 0, axis_index_groups=Z_GROUPS, tiled=True))
    own_sums, to_send = fold(place, held, second, [sums])
    far = swap(to_send, "y")
    q = quarter // 4

    gelu_share, slope = activate(place, own_sums, far)
    gelu_near = []
    for start, order in zip((0, q), TOKEN_ORDERS):
        two = jnp.concatenate([gelu_share[start : start + q], swap(gelu_share[start : start + q], order[1])])
        gelu_near += [two, swap(two, order[0])]
    gelu_keep = jnp.concatenate(gelu_near)
    pre_share = chain_slope(place, terms, slope, ())
    far = swap(pre_share, "y")
    two = [jnp.concatenate([pre_share[i : i + q], far[i : i + q]]) for i in (0, q)]

    pre_keep = [jnp.concatenate([t, swap(t, order[1])]) for t, order in zip(two, TOKEN_ORDERS)]

    gelu_keep, pre_keep = together(gelu_keep, pre_keep)
    cut = 11 * quarter // 8
    gelu_far = [swap(gelu_keep[:cut], "y")]
    pre_first = [swap(k, order[0]) for k, order in zip(pre_keep, TOKEN_ORDERS)]
    pre_keep_other = [swap(k, "core") for k in pre_keep]
    kept = input_sums(place, pre_keep, pre_keep_other, w_in)

    gelu_far[0], pre_first, kept, gelu_keep = together(gelu_far[0], pre_first, kept, gelu_keep)
    gelu_far.append(swap(gelu_keep[cut:], "y"))
    pre_first_other = [swap(f, "core") for f in pre_first]
    sums, w_in_grad = input_sums_and_grad(
        place,
        (*pre_keep, *pre_first),
        (*pre_keep_other, *pre_first_other),
        w_in,
        kept,
        tok_features,
    )
    parts = lax.all_to_all(sums, "row", 0, 0, tiled=True)
    w_in_grad, gelu_far[1] = together(w_in_grad, gelu_far[1])
    gelu_mine = (gelu_keep, *gelu_far)
    gelu_other = [swap(g, "core") for g in gelu_mine]
    w_out_grad = weight_grad(place, gelu_mine, gelu_other, grad_features)
    w_out_grad, parts = together(w_out_grad, parts)
    in_grad = input_total(place, parts)
    return (in_grad, w_in_grad, w_out_grad)


def solution(mesh):
    in_specs = (P("row", "col"), P("col", "row"), P("row", "col"), P("row", "col"))
    out_specs = (P("row", "col"), P("col", "row"), P("row", "col"))
    return jax.shard_map(body, mesh=mesh, in_specs=in_specs, out_specs=out_specs, check_vma=False)
```
